512 devices in a mesh: fsdp: 64 (over z, x_hi, core), tp: 8 (over y, x_lo).
Axes of the slice: x: 4 (x_hi: 2, x_lo: 2; x = x_hi * 2 + x_lo), y: 4, z: 16, core: 2. Of those that a mesh axis runs over, the one named last changes fastest.
Arguments:
- token_ids: int32 [256, 2], P('fsdp'), may hold values from 0 to 81919
- cache_lengths: int32 [256], P('fsdp'), may hold values from 256 to 1022, as said below
- embedding: bfloat16 [81920, 5120], P('fsdp', 'tp'), may hold values from -6 to 6
- norm_gain: bfloat16 [5120], replicated, may hold values from 0.099609375 to 1.8984375
- key_norm_gain: bfloat16 [128], replicated, may hold values from 0.099609375 to 1.8984375
- key_weight: float32 [5120, 1024], P(('fsdp', 'tp')), may hold values from -0.078125 to 0.078125
- key_grad: float32 [5120, 1024], P(('fsdp', 'tp')), may hold values from -12 to 12
- key_first: float32 [5120, 1024], P(('fsdp', 'tp')), may hold values from -1.2 to 1.2
- key_second: float32 [5120, 1024], P(('fsdp', 'tp')), may hold values from 0.5 to 8
- value_weight: float32 [5120, 1024], P(('fsdp', 'tp')), may hold values from -0.078125 to 0.078125
- value_grad: float32 [5120, 1024], P(('fsdp', 'tp')), may hold values from -12 to 12
- value_first: float32 [5120, 1024], P(('fsdp', 'tp')), may hold values from -1.2 to 1.2
- value_second: float32 [5120, 1024], P(('fsdp', 'tp')), may hold values from 0.5 to 8
- queries: bfloat16 [256, 2, 8192], P('fsdp', None, 'tp'), may hold values from -7 to 7
- key_cache: bfloat16 [256, 8, 1024, 128], P('fsdp', 'tp'), may hold values from -7 to 7
- cached_value_rows: bfloat16 [256, 8, 1024, 128], P('fsdp', 'tp'), may hold values from -6 to 6
Outputs:
- attention: bfloat16 [256, 2, 8192], P('fsdp', None, 'tp')
- new_key_weight: float32 [5120, 1024], P(('fsdp', 'tp'))
- new_key_first: float32 [5120, 1024], P(('fsdp', 'tp'))
- new_key_second: float32 [5120, 1024], P(('fsdp', 'tp'))
- new_value_weight: float32 [5120, 1024], P(('fsdp', 'tp'))
- new_value_first: float32 [5120, 1024], P(('fsdp', 'tp'))
- new_value_second: float32 [5120, 1024], P(('fsdp', 'tp'))
The draws below stay inside these ranges and needn't reach their ends.
Inputs may be any that keep to these rules, and one draw needn't show every extreme that they name: `cache_lengths`: cache entries at and above a rollout's length are unused; some rollout reaches the largest length.
All inputs are finite; a program needn't handle non-finite values.
Results may differ from the reference program's by a relative error of at most 0.0049.
Values may be sent and summed in bfloat16 or wider, within the bound.
No kernel may reach another device: no remote copies, remote signals or barrier semaphores. Data moves between devices by JAX's collectives and lax.ppermute only.
A program may use at most 64 MiB of HBM per device.

```python
import math
import jax
import jax.numpy as jnp
import numpy as np
from jax import lax

D = 5120
QUERY_HEADS = 64
KEY_VALUE_HEADS = 8
HEAD_SIZE = 128
KVW = 1024
VOCAB = 81920
ROLLOUT_COUNT = 256
CACHE_SLOTS = 1024


def draw_key_cache(key, part):
    key = jax.random.fold_in(key, 7)
    complete_shape = (ROLLOUT_COUNT, KEY_VALUE_HEADS, CACHE_SLOTS, HEAD_SIZE)
    values_drawn = jnp.clip(jax.random.normal(key, complete_shape, jnp.float32), -6.0, 6.0)
    return values_drawn.astype(jnp.bfloat16)


def draw_queries(key, part):
    key = jax.random.fold_in(key, 11)
    complete_shape = (ROLLOUT_COUNT, 2, QUERY_HEADS * HEAD_SIZE)
    values_drawn = jnp.clip(jax.random.normal(key, complete_shape, jnp.float32), -6.0, 6.0)
    return values_drawn.astype(jnp.bfloat16)


def draw_cache_lengths(key, part):
    key = jax.random.fold_in(key, 23)
    shortest = CACHE_SLOTS // 4
    lengths = jax.random.randint(jax.random.fold_in(key, 1), (ROLLOUT_COUNT,), shortest, CACHE_SLOTS - 1)
    longest = jax.random.randint(jax.random.fold_in(key, 3), (), 0, ROLLOUT_COUNT)
    lengths = jnp.where(jnp.arange(ROLLOUT_COUNT) == longest, CACHE_SLOTS - 2, lengths)
    return lengths.astype(jnp.int32)


def set_ends(drawn, key, least, top_value):
    spot = [jax.random.randint(jax.random.fold_in(key, axis), (), 0, length) for axis, length in enumerate(drawn.shape)]
    widest = drawn.shape.index(max(drawn.shape))
    next_to = spot[:widest] + [(spot[widest] + 1) % drawn.shape[widest]] + spot[widest + 1:]
    return drawn.at[tuple(spot)].set(least).at[tuple(next_to)].set(top_value)


def shard_levels(stream_key, dims, cuts, low, top_value):
    def one(position, parts):
        steps = jax.random.uniform(jax.random.fold_in(jax.random.fold_in(stream_key, 6), position), (parts,), jnp.float32, low / len(cuts), top_value / len(cuts))
        return jnp.repeat(jnp.exp(steps), dims[position] // parts).reshape((-1,) + (1,) * (len(dims) - position - 1))

    factor_of = one(*cuts[0])
    for cut in cuts[1:]:
        factor_of = factor_of * one(*cut)
    return factor_of


def skewed_wide(own_key, shape, number_of, slope):
    weights = [min(1 << octave, number_of + 1 - (1 << octave)) * (1 << 20) // math.isqrt((1 << octave) ** slope) + 1 for octave in range((number_of + 1).bit_length()) if 1 << octave <= number_of]
    spread = 1 + sum(weights) // (1 << 30)
    listing = np.cumsum(np.array([max(1, weight // spread) for weight in weights]))
    pick = jax.random.randint(jax.random.fold_in(own_key, 1), shape, 0, int(listing[len(weights) - 1]))
    start = jnp.left_shift(1, jnp.searchsorted(jnp.asarray(listing, jnp.int32), pick, side="right").astype(jnp.int32))
    rank = start - 1 + jax.random.randint(jax.random.fold_in(own_key, 4), shape, 0, 1 << 30) % jnp.minimum(start, number_of + 1 - start)
    return jax.random.permutation(jax.random.fold_in(own_key, 2), number_of)[rank].astype(jnp.int32)


def gaussian(rng, dims, scale, limit, shards=(), kind=jnp.bfloat16):
    result = scale * jax.random.normal(rng, dims, jnp.float32)
    if shards:
        result = result * shard_levels(rng, dims, shards, -0.22, 0.18)
    return jnp.clip(result, -limit, limit).astype(kind)


def setup_inputs(seed: int = 0) -> dict:
    seeds = jax.random.split(jax.random.key(seed), 17)
    return {
        "token_ids": set_ends(skewed_wide(seeds[0], (ROLLOUT_COUNT, 2), VOCAB, 2), jax.random.fold_in(seeds[0], 3), 0, VOCAB - 1).astype(jnp.int32),
        "cache_lengths": draw_cache_lengths(jax.random.fold_in(seeds[16], 71), 0),
        "embedding": gaussian(seeds[2], (VOCAB, D), 1.0, 6.0, ((0, 64), (1, 8))),
        "norm_gain": jnp.clip(1.0 + 0.18 * jax.random.normal(seeds[3], (D,), jnp.float32), 0.099609375, 1.8984375).astype(jnp.bfloat16),
        "key_norm_gain": jnp.clip(1.0 + 0.18 * jax.random.normal(seeds[4], (HEAD_SIZE,), jnp.float32), 0.099609375, 1.8984375).astype(jnp.bfloat16),
        "key_weight": gaussian(seeds[5], (D, KVW), D ** -0.5, 0.078125, ((0, 512),), jnp.float32),
        "key_grad": gaussian(seeds[6], (D, KVW), 2.0, 12.0, ((0, 512),), jnp.float32),
        "key_first": gaussian(seeds[7], (D, KVW), 0.2, 1.2, ((0, 512),), jnp.float32),
        "key_second": jnp.clip(jnp.exp(math.log(8.0) - 2.7725887 * jax.random.uniform(seeds[8], (D, KVW), jnp.float32) ** shard_levels(seeds[8], (D, KVW), ((0, 512),), -0.2, 0.2)), 0.5, 8.0),
        "value_weight": gaussian(seeds[9], (D, KVW), D ** -0.5, 0.078125, ((0, 512),), jnp.float32),
        "value_grad": gaussian(seeds[10], (D, KVW), 2.0, 12.0, ((0, 512),), jnp.float32),
        "value_first": gaussian(seeds[11], (D, KVW), 0.2, 1.2, ((0, 512),), jnp.float32),
        "value_second": jnp.clip(jnp.exp(math.log(8.0) - 2.7725887 * jax.random.uniform(seeds[12], (D, KVW), jnp.float32) ** shard_levels(seeds[12], (D, KVW), ((0, 512),), -0.2, 0.2)), 0.5, 8.0),
        "queries": draw_queries(jax.random.fold_in(seeds[16], 71), 0),
        "key_cache": draw_key_cache(jax.random.fold_in(seeds[16], 71), 0),
        "cached_value_rows": gaussian(seeds[15], (ROLLOUT_COUNT, KEY_VALUE_HEADS, CACHE_SLOTS, HEAD_SIZE), 1.0, 6.0, ((0, 64), (1, 8))),
    }


beta_one = 0.9
beta_two = 0.95
learn_rate = 0.001
weight_decay = 0.1
adam_eps = 1e-08
norm_eps = 1e-06
rope_base = 1000000.0

def adamw(weight, gradient, moment_one, moment_two):
    first_new = beta_one * moment_one + (1.0 - beta_one) * gradient
    second_new = beta_two * moment_two + (1.0 - beta_two) * gradient * gradient
    correct_one = 1.0 - beta_one ** 50
    correct_two = 1.0 - beta_two ** 50
    update = first_new / correct_one / (jnp.sqrt(second_new / correct_two) + adam_eps) + weight_decay * weight
    return (weight - learn_rate * update, first_new, second_new)

def rotate(vectors, positions):
    half_width = vectors.shape[-1] // 2
    frequency = rope_base ** (-jnp.arange(half_width, dtype=jnp.float32) * 2.0 / vectors.shape[-1])
    angles = positions[..., None] * frequency
    cosine = jnp.cos(angles)
    sine = jnp.sin(angles)
    upper_half = vectors[..., :half_width]
    lower_half = vectors[..., half_width:]
    return jnp.concatenate([upper_half * cosine - lower_half * sine, lower_half * cosine + upper_half * sine], axis=-1)

def attend_one(inputs):
    single_query_row, cache_keys, cache_values, fresh_keys, fresh_values, length = inputs
    head_groups = QUERY_HEADS // KEY_VALUE_HEADS
    score_scale = HEAD_SIZE ** (-0.5)
    heads_of_query = single_query_row.astype(jnp.float32).reshape(2, KEY_VALUE_HEADS, head_groups, HEAD_SIZE)
    cache_scores = jnp.einsum('skgd,kcd->skgc', heads_of_query, cache_keys.astype(jnp.float32)) * score_scale
    valid_cache = jnp.arange(CACHE_SLOTS, dtype=jnp.int32) < length
    cache_scores = jnp.where(valid_cache[None, None, None, :], cache_scores, -jnp.inf)
    fresh_scores = jnp.einsum('skgd,tkd->skgt', heads_of_query, fresh_keys.astype(jnp.float32)) * score_scale
    causal = jnp.arange(2)[None, :] <= jnp.arange(2)[:, None]
    fresh_scores = jnp.where(causal[:, None, None, :], fresh_scores, -jnp.inf)
    highest = jnp.maximum(lax.optimization_barrier(jnp.max(cache_scores, axis=-1)), lax.optimization_barrier(jnp.max(fresh_scores, axis=-1)))
    cache_exp = jnp.exp(cache_scores - highest[..., None])
    fresh_exp = jnp.exp(fresh_scores - highest[..., None])
    denominator = lax.optimization_barrier(jnp.sum(cache_exp, axis=-1)) + lax.optimization_barrier(jnp.sum(fresh_exp, axis=-1))
    cache_share = (cache_exp / denominator[..., None]).astype(jnp.bfloat16)
    fresh_share = (fresh_exp / denominator[..., None]).astype(jnp.bfloat16)
    mixed = jnp.einsum('skgc,kcd->skgd', cache_share.astype(jnp.float32), cache_values.astype(jnp.float32))
    mixed = mixed + jnp.einsum('skgt,tkd->skgd', fresh_share.astype(jnp.float32), fresh_values.astype(jnp.float32))
    return mixed.reshape(2, QUERY_HEADS * HEAD_SIZE).astype(jnp.bfloat16)

def reference(token_ids, cache_lengths, embedding, norm_gain, key_norm_gain, key_weight, key_grad, key_first, key_second, value_weight, value_grad, value_first, value_second, queries, key_cache, cached_value_rows):
    new_key_weight, new_key_first, new_key_second = adamw(key_weight, key_grad, key_first, key_second)
    new_value_weight, new_value_first, new_value_second = adamw(value_weight, value_grad, value_first, value_second)
    rollout_key = new_key_weight.astype(jnp.bfloat16)
    rollout_value = new_value_weight.astype(jnp.bfloat16)
    embedded = embedding[token_ids.reshape(-1)]
    widened = embedded.astype(jnp.float32)
    normed = (widened * lax.rsqrt(lax.optimization_barrier(jnp.mean(widened * widened, axis=-1, keepdims=True)) + norm_eps) * norm_gain.astype(jnp.float32)).astype(jnp.bfloat16)
    key_projector = jnp.dot(normed, rollout_key, preferred_element_type=jnp.float32)
    value_projector = jnp.dot(normed, rollout_value, preferred_element_type=jnp.float32)
    heads_of_key = key_projector.reshape(ROLLOUT_COUNT, 2, KEY_VALUE_HEADS, HEAD_SIZE)
    key_normed = heads_of_key * lax.rsqrt(lax.optimization_barrier(jnp.mean(heads_of_key * heads_of_key, axis=-1, keepdims=True)) + norm_eps) * key_norm_gain.astype(jnp.float32)
    positions = (cache_lengths[:, None] + jnp.arange(2, dtype=jnp.int32)[None, :]).astype(jnp.float32)
    new_keys = rotate(key_normed, positions[:, :, None]).astype(jnp.bfloat16)
    incoming_values = value_projector.reshape(ROLLOUT_COUNT, 2, KEY_VALUE_HEADS, HEAD_SIZE).astype(jnp.bfloat16)
    attention = lax.map(attend_one, (queries, key_cache, cached_value_rows, new_keys, incoming_values, cache_lengths))
    return (attention, new_key_weight, new_key_first, new_key_second, new_value_weight, new_value_first, new_value_second)
```

```python
import jax
import jax.numpy as jnp
from jax import lax
from jax.sharding import Mesh, PartitionSpec as P

HEAD_SIZE = 128


beta_one = 0.9
beta_two = 0.95
learn_rate = 0.001
weight_decay = 0.1
adam_eps = 1e-08
norm_eps = 1e-06
rope_base = 1000000.0


def adamw(weight, gradient, moment_one, moment_two):
    first_new = beta_one * moment_one + (1.0 - beta_one) * gradient
    second_new = beta_two * moment_two + (1.0 - beta_two) * gradient * gradient
    correct_one = 1.0 - beta_one**50
    correct_two = 1.0 - beta_two**50
    update = (
        first_new / correct_one / (jnp.sqrt(second_new / correct_two) + adam_eps)
        + weight_decay * weight
    )
    return (weight - learn_rate * update, first_new, second_new)


def rotate(vectors, positions):
    half_width = vectors.shape[-1] // 2
    frequency = rope_base ** (-jnp.arange(half_width, dtype=jnp.float32) * 2.0 / vectors.shape[-1])
    angles = positions[..., None] * frequency
    cosine = jnp.cos(angles)
    sine = jnp.sin(angles)
    upper_half = vectors[..., :half_width]
    lower_half = vectors[..., half_width:]
    return jnp.concatenate(
        [upper_half * cosine - lower_half * sine, lower_half * cosine + upper_half * sine], axis=-1
    )


def body(
    token_ids,
    cache_lengths,
    embedding,
    norm_gain,
    key_norm_gain,
    key_weight,
    key_grad,
    key_first,
    key_second,
    value_weight,
    value_grad,
    value_first,
    value_second,
    queries,
    key_cache,
    cached_value_rows,
):
    rollouts = token_ids.shape[0]
    tokens = 2 * rollouts
    z_size, quad_size, tp_size = lax.axis_size(Z), lax.axis_size(QUAD), lax.axis_size(TP)
    fsdp_size = z_size * quad_size

    own_ids = jnp.broadcast_to(token_ids.reshape(1, tokens), (fsdp_size, tokens))
    all_ids = lax.all_to_all(own_ids, FSDP, split_axis=0, concat_axis=0, tiled=False)

    new_key_weight, new_key_first, new_key_second = adamw(
        key_weight, key_grad, key_first, key_second
    )
    new_value_weight, new_value_first, new_value_second = adamw(
        value_weight, value_grad, value_first, value_second
    )
    own_rows = key_weight.shape[0]
    both = jnp.stack(
        [
            new_key_weight.astype(jnp.bfloat16).reshape(own_rows, tp_size, HEAD_SIZE),
            new_value_weight.astype(jnp.bfloat16).reshape(own_rows, tp_size, HEAD_SIZE),
        ],
        axis=2,
    ).reshape(own_rows, tp_size, 2 * HEAD_SIZE)
    head_rows = lax.all_to_all(
        both.transpose(1, 0, 2), TP, split_axis=0, concat_axis=0, tiled=False
    ).reshape(tp_size * own_rows, 2 * HEAD_SIZE)
    quad_rows = lax.all_gather(head_rows, QUAD, axis=0, tiled=True)
    projections = lax.all_gather(quad_rows, Z, axis=0, tiled=True)

    vocab_rows, features = embedding.shape
    ordered = all_ids.reshape(z_size, quad_size, tokens).transpose(1, 0, 2).reshape(-1)
    local_ids = ordered - lax.axis_index(FSDP) * vocab_rows
    vocab_index = jnp.arange(vocab_rows, dtype=jnp.int32)
    onehot = (local_ids[:, None] == vocab_index[None, :]).astype(jnp.bfloat16)
    found = jnp.dot(onehot, embedding, preferred_element_type=jnp.float32).astype(jnp.bfloat16)
    found = found.reshape(quad_size, z_size * tokens, features)
    found = lax.all_to_all(found, QUAD, split_axis=0, concat_axis=0, tiled=False)
    found = jnp.sum(found.astype(jnp.float32), axis=0).astype(jnp.bfloat16)
    found = found.reshape(z_size, tokens, features)
    found = lax.all_to_all(found, Z, split_axis=0, concat_axis=0, tiled=False)
    found = jnp.sum(found.astype(jnp.float32), axis=0).astype(jnp.bfloat16)
    found = jnp.broadcast_to(found[None], (tp_size, tokens, features))
    found = lax.all_to_all(found, TP, split_axis=0, concat_axis=0, tiled=False)
    embedded = found.transpose(1, 0, 2).reshape(tokens, tp_size * features)

    widened = embedded.astype(jnp.float32)
    normed = (
        widened
        * lax.rsqrt(jnp.mean(widened * widened, axis=-1, keepdims=True) + norm_eps)
        * norm_gain.astype(jnp.float32)
    ).astype(jnp.bfloat16)
    projected = jnp.dot(normed, projections, preferred_element_type=jnp.float32)
    heads_of_key = projected[:, :HEAD_SIZE].reshape(rollouts, 2, HEAD_SIZE)
    key_normed = (
        heads_of_key
        * lax.rsqrt(jnp.mean(heads_of_key * heads_of_key, axis=-1, keepdims=True) + norm_eps)
        * key_norm_gain.astype(jnp.float32)
    )
    positions = (cache_lengths[:, None] + jnp.arange(2, dtype=jnp.int32)[None, :]).astype(
        jnp.float32
    )
    new_keys = rotate(key_normed, positions).astype(jnp.bfloat16)
    new_values = projected[:, HEAD_SIZE:].reshape(rollouts, 2, HEAD_SIZE).astype(jnp.bfloat16)

    groups = queries.shape[2] // HEAD_SIZE
    slots = key_cache.shape[2]
    score_scale = HEAD_SIZE ** (-0.5)
    rows = queries.reshape(rollouts, 2 * groups, HEAD_SIZE)
    cache_scores = (
        jnp.einsum("rqd,rcd->rqc", rows, key_cache[:, 0], preferred_element_type=jnp.float32)
        * score_scale
    )
    valid_cache = jnp.arange(slots, dtype=jnp.int32)[None, :] < cache_lengths[:, None]
    cache_scores = jnp.where(valid_cache[:, None, :], cache_scores, -jnp.inf)
    cache_highest = jnp.max(cache_scores, axis=-1, keepdims=True)
    cache_exp = jnp.exp(cache_scores - cache_highest)
    cache_sum = jnp.sum(cache_exp, axis=-1, keepdims=True)
    cache_mixed = jnp.einsum(
        "rqc,rcd->rqd",
        cache_exp.astype(jnp.bfloat16),
        cached_value_rows[:, 0],
        preferred_element_type=jnp.float32,
    )

    fresh_scores = (
        jnp.einsum("rqd,rtd->rqt", rows, new_keys, preferred_element_type=jnp.float32)
        * score_scale
    )
    step = jnp.arange(2 * groups) // groups
    causal = jnp.arange(2)[None, :] <= step[:, None]
    fresh_scores = jnp.where(causal[None], fresh_scores, -jnp.inf)
    highest = jnp.maximum(cache_highest, jnp.max(fresh_scores, axis=-1, keepdims=True))
    cache_factor = jnp.exp(cache_highest - highest)
    fresh_exp = jnp.exp(fresh_scores - highest)
    denominator = cache_sum * cache_factor + jnp.sum(fresh_exp, axis=-1, keepdims=True)
    mixed = cache_mixed * cache_factor + jnp.einsum(
        "rqt,rtd->rqd",
        fresh_exp.astype(jnp.bfloat16),
        new_values,
        preferred_element_type=jnp.float32,
    )
    attention = (mixed / denominator).reshape(rollouts, 2, queries.shape[2]).astype(jnp.bfloat16)
    return (
        attention,
        new_key_weight,
        new_key_first,
        new_key_second,
        new_value_weight,
        new_value_first,
        new_value_second,
    )


Z = "z"
QUAD = ("xh", "core")
FSDP = ("z", "xh", "core")
TP = "tp"


def solution(mesh):
    fine = Mesh(mesh.devices.reshape(16, 2, 2, 8), ("z", "xh", "core", "tp"))
    rows = P(FSDP + (TP,), None)
    placed = (
        P(FSDP, None),
        P(FSDP),
        P(FSDP, TP),
        P(),
        P(),
        *[rows] * 8,
        P(FSDP, None, TP),
        P(FSDP, TP, None, None),
        P(FSDP, TP, None, None),
    )
    return jax.shard_map(
        body,
        mesh=fine,
        in_specs=placed,
        out_specs=(P(FSDP, None, TP), *[rows] * 6),
        check_vma=False,
    )
```

```python
import jax
import jax.numpy as jnp
from jax import lax
from jax.experimental import pallas as pl
from jax.experimental.pallas import tpu as pltpu
from jax.sharding import Mesh
from jax.sharding import PartitionSpec as P

HEAD_SIZE = 128
LANES = 128
BLOCK_ROWS = 40
BLOCK = 48
CHUNK = 384
HIGH_COLUMN = 40
LOW_COLUMN = 41


beta_one = 0.9
beta_two = 0.95
learn_rate = 0.001
weight_decay = 0.1
adam_eps = 1e-08
norm_eps = 1e-06
rope_base = 1000000.0


def adamw(weight, gradient, moment_one, moment_two):
    first_new = beta_one * moment_one + (1.0 - beta_one) * gradient
    second_new = beta_two * moment_two + (1.0 - beta_two) * gradient * gradient
    correct_one = 1.0 - beta_one**50
    correct_two = 1.0 - beta_two**50
    update = (
        first_new / correct_one / (jnp.sqrt(second_new / correct_two) + adam_eps)
        + weight_decay * weight
    )
    return (weight - learn_rate * update, first_new, second_new)


def call(kernel, shape, dtype, *operands):
    return pl.pallas_call(
        kernel,
        out_shape=jax.ShapeDtypeStruct(shape, dtype),
        compiler_params=pltpu.CompilerParams(vmem_limit_bytes=16 * 1024 * 1024),
    )(*operands)


def look_up(ids_ref, table_ref, other_ref, sort_ref, found_ref):
    count = ids_ref.shape[1]
    eye = lax.broadcasted_iota(jnp.int32, (count, count), 0) == lax.broadcasted_iota(
        jnp.int32, (count, count), 1
    )
    total = jnp.zeros((count, table_ref.shape[1]), jnp.float32)
    for part, held in enumerate((table_ref, other_ref)):
        row = jnp.broadcast_to(ids_ref[part : part + 1, :], (count, count))
        ids = jnp.sum(jnp.where(eye, row, 0), axis=1, keepdims=True)
        index = lax.broadcasted_iota(jnp.int32, (count, held.shape[0]), 1)
        onehot = jnp.where(ids == index, 1.0, 0.0).astype(jnp.bfloat16)
        total += jnp.dot(onehot, held[...], preferred_element_type=jnp.float32)
    found_ref[...] = jnp.dot(
        total.astype(jnp.bfloat16), sort_ref[...], preferred_element_type=jnp.float32
    ).astype(jnp.bfloat16)


def split_rows(came_ref, chunks_ref):
    total = came_ref[0].astype(jnp.float32) + came_ref[1].astype(jnp.float32)
    squares = jnp.sum(jnp.sum(total * total, axis=0), axis=-1, keepdims=True)
    high = squares.astype(jnp.bfloat16).astype(jnp.float32)
    low = squares - high
    column = lax.broadcasted_iota(jnp.int32, (squares.shape[0], CHUNK), 1)
    extra = jnp.where(column == HIGH_COLUMN, high, jnp.where(column == LOW_COLUMN, low, 0.0))
    for place in range(total.shape[0]):
        for half in range(2):
            chunk = total[place, :, half * CHUNK : (half + 1) * CHUNK] + extra
            chunks_ref[2 * place + half] = chunk.astype(jnp.bfloat16)


def pack(came_ref, weight_ref, packed_ref):
    rows = jnp.sum(came_ref[...].astype(jnp.float32), axis=0).astype(jnp.bfloat16)
    count = rows.shape[0]
    parts = CHUNK // LANES
    for place in range(packed_ref.shape[0]):
        for part in range(parts):
            packed_ref[place, part * count : (part + 1) * count, :] = rows[
                :, part * LANES : (part + 1) * LANES
            ]
        packed_ref[place, parts * count : parts * count + BLOCK, :] = weight_ref[place, :, :LANES]
        packed_ref[place, parts * count + BLOCK :, :] = weight_ref[place, :, LANES:]


def project(came_ref, gain_ref, product_ref):
    places = came_ref.shape[0]
    parts = CHUNK // LANES
    count = (came_ref.shape[1] - 2 * BLOCK) // parts
    rows = [
        came_ref[:, part * count : (part + 1) * count, :]
        .reshape(places * count, LANES)
        .astype(jnp.float32)
        for part in range(parts)
    ]
    column = lax.broadcasted_iota(jnp.int32, rows[0].shape, 1)
    marked = (column == HIGH_COLUMN) | (column == LOW_COLUMN)
    squares = jnp.sum(jnp.where(marked, rows[0], 0.0), axis=-1, keepdims=True)
    factor = lax.rsqrt(squares / FEATURES + norm_eps)
    normed = jnp.concatenate(
        [
            (rows[part] * factor * gain_ref[:, part * LANES : (part + 1) * LANES]).astype(
                jnp.bfloat16
            )
            for part in range(parts)
        ],
        axis=1,
    )
    for side in range(2):
        start = parts * count + side * BLOCK
        weight = came_ref[:, start : start + BLOCK, :].reshape(places * BLOCK, LANES)
        product = jnp.dot(normed, weight, preferred_element_type=jnp.float32)
        product_ref[:, :, side * LANES : (side + 1) * LANES] = product.reshape(
            product_ref.shape[0], product_ref.shape[1], LANES
        )


def finish(
    came_ref, gain_ref, cosine_ref, sine_ref, query_ref, mixed_ref, highest_ref, sum_ref, out_ref
):
    total = jnp.sum(came_ref[...], axis=0)
    keys = total[:, :LANES]
    values = total[:, LANES:].astype(jnp.bfloat16)
    factor = lax.rsqrt(jnp.mean(keys * keys, axis=-1, keepdims=True) + norm_eps)
    keys = keys * factor * gain_ref[...]
    turned = jnp.concatenate([keys[:, LANES // 2 :], keys[:, : LANES // 2]], axis=1)
    keys = (keys * cosine_ref[...] + turned * sine_ref[...]).astype(jnp.bfloat16)
    count = query_ref.shape[0]
    fresh = lax.dot_general(
        query_ref[...], keys, (((1,), (1,)), ((), ())), preferred_element_type=jnp.float32
    ) * (HEAD_SIZE**-0.5)
    row = lax.broadcasted_iota(jnp.int32, fresh.shape, 0)
    column = lax.broadcasted_iota(jnp.int32, fresh.shape, 1)
    each = count // (keys.shape[0] // 2)
    step = row % each // (each // 2)
    joined = (row // each == column // 2) & (column % 2 <= step)
    fresh = jnp.where(joined, fresh, -jnp.inf)
    highest = jnp.maximum(highest_ref[...], jnp.max(fresh, axis=-1, keepdims=True))
    weights = jnp.exp(fresh - highest)
    factor = jnp.exp(highest_ref[...] - highest)
    denominator = sum_ref[...] * factor + jnp.sum(weights, axis=-1, keepdims=True)
    mixed = mixed_ref[...] * factor + jnp.dot(
        weights,
        values.astype(jnp.float32),
        precision=lax.Precision.HIGHEST,
        preferred_element_type=jnp.float32,
    )
    mixed = (mixed / denominator).astype(jnp.bfloat16)
    groups = each // 2
    for at in range(2 * out_ref.shape[0]):
        for group in range(groups):
            out_ref[at // 2, at % 2 : at % 2 + 1, group * HEAD_SIZE : (group + 1) * HEAD_SIZE] = (
                mixed[at * groups + group : at * groups + group + 1, :]
            )


FEATURES = 5120


def body(
    token_ids,
    cache_lengths,
    embedding,
    norm_gain,
    key_norm_gain,
    key_weight,
    key_grad,
    key_first,
    key_second,
    value_weight,
    value_grad,
    value_first,
    value_second,
    queries,
    key_cache,
    cached_value_rows,
):
    rollouts = token_ids.shape[0]
    tokens = 2 * rollouts
    z_size, quad_size, tp_size = lax.axis_size("z"), lax.axis_size(QUAD), lax.axis_size(TP)
    own_rows = key_weight.shape[0]
    vocab_rows, features = embedding.shape

    chips = z_size * lax.axis_size("xh")
    own_ids = jnp.broadcast_to(token_ids.reshape(1, tokens), (chips, tokens))
    all_ids = lax.all_to_all(own_ids, ("xh", "z"), split_axis=0, concat_axis=0, tiled=False)

    column = jnp.arange(2 * CHUNK, dtype=jnp.int32)
    half, place = column // CHUNK, column % CHUNK // BLOCK
    row = column % BLOCK
    feature = half * (features // 2) + (row // own_rows * tp_size + place) * own_rows + row % own_rows
    feature = jnp.where(row < BLOCK_ROWS, feature, -1)
    sort = (jnp.arange(features, dtype=jnp.int32)[:, None] == feature[None, :]).astype(jnp.bfloat16)
    other_table = lax.ppermute(embedding, "core", [(0, 1), (1, 0)])

    new_key_weight, new_key_first, new_key_second = adamw(
        key_weight, key_grad, key_first, key_second
    )
    new_value_weight, new_value_first, new_value_second = adamw(
        value_weight, value_grad, value_first, value_second
    )
    both = jnp.stack(
        [
            new_key_weight.astype(jnp.bfloat16).reshape(own_rows, tp_size, HEAD_SIZE),
            new_value_weight.astype(jnp.bfloat16).reshape(own_rows, tp_size, HEAD_SIZE),
        ],
        axis=2,
    ).reshape(own_rows, 2 * tp_size * HEAD_SIZE)
    quad_rows = lax.all_gather(both, QUAD, axis=0, tiled=False)
    quad_rows = quad_rows.reshape(quad_size * own_rows, tp_size, 2 * HEAD_SIZE).transpose(1, 0, 2)
    quad_rows = jnp.pad(quad_rows, ((0, 0), (0, BLOCK - BLOCK_ROWS), (0, 0)))

    all_ids, quad_rows = lax.optimization_barrier((all_ids, quad_rows))

    gain = jnp.dot(
        norm_gain.reshape(z_size, -1), sort[: features // 2, :CHUNK], preferred_element_type=jnp.float32
    )
    gain = lax.dynamic_slice_in_dim(gain, lax.axis_index("z"), 1, axis=0)

    groups = queries.shape[2] // HEAD_SIZE
    slots = key_cache.shape[2]
    score_scale = HEAD_SIZE ** (-0.5)
    rows = queries.reshape(rollouts, 2 * groups, HEAD_SIZE)
    cache_scores = (
        jnp.einsum("rqd,rcd->rqc", rows, key_cache[:, 0], preferred_element_type=jnp.float32)
        * score_scale
    )
    valid_cache = jnp.arange(slots, dtype=jnp.int32)[None, :] < cache_lengths[:, None]
    cache_scores = jnp.where(valid_cache[:, None, :], cache_scores, -jnp.inf)
    cache_highest = jnp.max(cache_scores, axis=-1, keepdims=True)
    cache_exp = jnp.exp(cache_scores - cache_highest)
    cache_sum = jnp.sum(cache_exp, axis=-1, keepdims=True)
    high = cache_exp.astype(jnp.bfloat16)
    low = (cache_exp - high.astype(jnp.float32)).astype(jnp.bfloat16)
    cache_mixed = jnp.einsum(
        "rqc,rcd->rqd",
        jnp.concatenate([high, low], axis=1),
        cached_value_rows[:, 0],
        preferred_element_type=jnp.float32,
    )
    cache_mixed = cache_mixed[:, : 2 * groups] + cache_mixed[:, 2 * groups :]

    positions = (cache_lengths[:, None] + jnp.arange(2, dtype=jnp.int32)[None, :]).astype(
        jnp.float32
    )
    frequency = rope_base ** (
        -jnp.arange(HEAD_SIZE // 2, dtype=jnp.float32) * 2.0 / HEAD_SIZE
    )
    angles = positions.reshape(tokens, 1) * frequency
    cosine, sine = jnp.cos(angles), jnp.sin(angles)
    cosine = jnp.concatenate([cosine, cosine], axis=1)
    sine = jnp.concatenate([-sine, sine], axis=1)

    part = lax.axis_index(FSDP)
    owners = jnp.stack([part, part ^ 1])
    ids = all_ids.reshape(1, -1) - owners[:, None] * vocab_rows
    found = call(
        look_up, (ids.shape[1], 2 * CHUNK), jnp.bfloat16, ids, embedding, other_table, sort
    )
    each = 2 * tokens
    found = found.reshape(-1, each, 2 * CHUNK)
    found = lax.all_to_all(found, ("xh", TP), split_axis=0, concat_axis=0, tiled=False)
    found = found.reshape(2, tp_size, each, 2 * CHUNK)
    found = call(split_rows, (z_size, each, CHUNK), jnp.bfloat16, found)
    found = lax.all_to_all(found, "z", split_axis=0, concat_axis=0, tiled=False)
    message_rows = CHUNK // LANES * each + 2 * BLOCK
    packed = call(pack, (tp_size, message_rows, LANES), jnp.bfloat16, found, quad_rows)
    packed = lax.all_to_all(packed, TP, split_axis=0, concat_axis=0, tiled=False)
    product = call(project, (z_size, tokens, 2 * HEAD_SIZE), jnp.float32, packed, gain)
    product = lax.all_to_all(product, "z", split_axis=0, concat_axis=0, tiled=False)
    attention = call(
        finish,
        queries.shape,
        jnp.bfloat16,
        product,
        key_norm_gain.astype(jnp.float32).reshape(1, HEAD_SIZE),
        cosine,
        sine,
        rows.reshape(-1, HEAD_SIZE),
        cache_mixed.reshape(-1, HEAD_SIZE),
        cache_highest.reshape(-1, 1),
        cache_sum.reshape(-1, 1),
    )
    return (
        attention,
        new_key_weight,
        new_key_first,
        new_key_second,
        new_value_weight,
        new_value_first,
        new_value_second,
    )


QUAD = ("xh", "core")
FSDP = ("z", "xh", "core")
TP = "tp"


def solution(mesh):
    fine = Mesh(mesh.devices.reshape(16, 2, 2, 8), ("z", "xh", "core", "tp"))
    rows = P(FSDP + (TP,), None)
    placed = (
        P(FSDP, None),
        P(FSDP),
        P(FSDP, TP),
        P(),
        P(),
        *[rows] * 8,
        P(FSDP, None, TP),
        P(FSDP, TP, None, None),
        P(FSDP, TP, None, None),
    )
    return jax.shard_map(
        body,
        mesh=fine,
        in_specs=placed,
        out_specs=(P(FSDP, None, TP), *[rows] * 6),
        check_vma=False,
    )
```

```python
import jax
import jax.numpy as jnp
from jax import lax
from jax.experimental import pallas as pl
from jax.experimental.pallas import tpu as pltpu
from jax.sharding import Mesh
from jax.sharding import PartitionSpec as P

HEAD_SIZE = 128
LANES = 128
BLOCK_ROWS = 40
BLOCK = 48
CHUNK = 384
OWN_ROWS = 10
COVER_FLOPS = 20_000_000_000
COVER_BYTES = 60_000_000
HIGH_COLUMN = 40
LOW_COLUMN = 41


beta_one = 0.9
beta_two = 0.95
learn_rate = 0.001
weight_decay = 0.1
adam_eps = 1e-08
norm_eps = 1e-06
rope_base = 1000000.0


def adamw(weight, gradient, moment_one, moment_two):
    first_new = beta_one * moment_one + (1.0 - beta_one) * gradient
    second_new = beta_two * moment_two + (1.0 - beta_two) * gradient * gradient
    correct_one = 1.0 - beta_one**50
    correct_two = 1.0 - beta_two**50
    update = (
        first_new / correct_one / (jnp.sqrt(second_new / correct_two) + adam_eps)
        + weight_decay * weight
    )
    return (weight - learn_rate * update, first_new, second_new)


def call(kernel, shape, dtype, *operands):
    return pl.pallas_call(
        kernel,
        out_shape=jax.ShapeDtypeStruct(shape, dtype),
        compiler_params=pltpu.CompilerParams(vmem_limit_bytes=16 * 1024 * 1024),
    )(*operands)


def look_up(row_ref, table_ref, other_ref, found_ref):
    count = row_ref.shape[1]
    eye = lax.broadcasted_iota(jnp.int32, (count, count), 0) == lax.broadcasted_iota(
        jnp.int32, (count, count), 1
    )
    row = jnp.broadcast_to(row_ref[...], (count, count))
    row = jnp.sum(jnp.where(eye, row, 0), axis=1, keepdims=True)
    size = table_ref.shape[0]
    index = lax.broadcasted_iota(jnp.int32, (count, size), 1)
    own = jnp.where(row == index, 1.0, 0.0).astype(jnp.bfloat16)
    other = jnp.where(row - size == index, 1.0, 0.0).astype(jnp.bfloat16)
    total = jnp.dot(own, table_ref[...], preferred_element_type=jnp.float32)
    total += jnp.dot(other, other_ref[...], preferred_element_type=jnp.float32)
    found_ref[...] = total.astype(jnp.bfloat16)


def update(*refs):
    given, new, both_ref = refs[:8], refs[8:14], refs[14]
    for side in range(2):
        results = adamw(*[ref[...] for ref in given[4 * side : 4 * side + 4]])
        for ref, result in zip(new[3 * side : 3 * side + 3], results):
            ref[...] = result
        rounded = results[0].astype(jnp.bfloat16)
        for place in range(rounded.shape[1] // HEAD_SIZE):
            start = (2 * place + side) * HEAD_SIZE
            both_ref[:, start : start + HEAD_SIZE] = rounded[
                :, place * HEAD_SIZE : (place + 1) * HEAD_SIZE
            ]


def sort_columns(sort_ref):
    features = sort_ref.shape[0]
    column = lax.broadcasted_iota(jnp.int32, sort_ref.shape, 1)
    half, place, row = column // CHUNK, column % CHUNK // BLOCK, column % BLOCK
    quad, own = row // OWN_ROWS, row % OWN_ROWS
    feature = half * (features // 2) + (quad * (CHUNK // BLOCK) + place) * OWN_ROWS + own
    held = lax.broadcasted_iota(jnp.int32, sort_ref.shape, 0)
    chosen = (held == feature) & (row < BLOCK_ROWS)
    sort_ref[...] = jnp.where(chosen, 1.0, 0.0).astype(jnp.bfloat16)


def split_rows(came_ref, sort_ref, chunks_ref):
    total = came_ref[0].astype(jnp.float32) + came_ref[1].astype(jnp.float32)
    places, count, features = total.shape
    squares = jnp.sum(jnp.sum(total * total, axis=0), axis=-1, keepdims=True)
    high = squares.astype(jnp.bfloat16).astype(jnp.float32)
    low = squares - high
    column = lax.broadcasted_iota(jnp.int32, (count, CHUNK), 1)
    extra = jnp.where(column == HIGH_COLUMN, high, jnp.where(column == LOW_COLUMN, low, 0.0))
    total = total.reshape(places * count, features).astype(jnp.bfloat16)
    total = jnp.dot(total, sort_ref[...], preferred_element_type=jnp.float32)
    total = total.reshape(places, count, 2 * CHUNK)
    for place in range(places):
        for half in range(2):
            chunk = total[place, :, half * CHUNK : (half + 1) * CHUNK] + extra
            chunks_ref[2 * place + half] = chunk.astype(jnp.bfloat16)


def pack(came_ref, weight_ref, packed_ref):
    rows = jnp.sum(came_ref[...].astype(jnp.float32), axis=0).astype(jnp.bfloat16)
    count = rows.shape[0]
    parts = CHUNK // LANES
    for place in range(packed_ref.shape[0]):
        for part in range(parts):
            packed_ref[place, part * count : (part + 1) * count, :] = rows[
                :, part * LANES : (part + 1) * LANES
            ]
        packed_ref[place, parts * count : parts * count + BLOCK, :] = weight_ref[place, :, :LANES]
        packed_ref[place, parts * count + BLOCK :, :] = weight_ref[place, :, LANES:]


def project(came_ref, gain_ref, product_ref):
    places = came_ref.shape[0]
    parts = CHUNK // LANES
    count = (came_ref.shape[1] - 2 * BLOCK) // parts
    rows = [
        came_ref[:, part * count : (part + 1) * count, :]
        .reshape(places * count, LANES)
        .astype(jnp.float32)
        for part in range(parts)
    ]
    column = lax.broadcasted_iota(jnp.int32, rows[0].shape, 1)
    marked = (column == HIGH_COLUMN) | (column == LOW_COLUMN)
    squares = jnp.sum(jnp.where(marked, rows[0], 0.0), axis=-1, keepdims=True)
    factor = lax.rsqrt(squares / FEATURES + norm_eps)
    normed = jnp.concatenate(
        [
            (rows[part] * factor * gain_ref[:, part * LANES : (part + 1) * LANES]).astype(
                jnp.bfloat16
            )
            for part in range(parts)
        ],
        axis=1,
    )
    products = []
    for side in range(2):
        start = parts * count + side * BLOCK
        weight = came_ref[:, start : start + BLOCK, :].reshape(places * BLOCK, LANES)
        product = jnp.dot(normed, weight, preferred_element_type=jnp.float32)
        products.append(product.reshape(product_ref.shape[0], product_ref.shape[1] // 2, LANES))
    product_ref[...] = jnp.concatenate(products, axis=1).astype(jnp.bfloat16)


def finish(
    came_ref, gain_ref, cosine_ref, sine_ref, query_ref, mixed_ref, highest_ref, sum_ref, out_ref
):
    total = jnp.sum(came_ref[...].astype(jnp.float32), axis=0)
    tokens = total.shape[0] // 2
    keys = total[:tokens]
    values = total[tokens:].astype(jnp.bfloat16)
    factor = lax.rsqrt(jnp.mean(keys * keys, axis=-1, keepdims=True) + norm_eps)
    keys = keys * factor * gain_ref[...]
    turned = jnp.concatenate([keys[:, LANES // 2 :], keys[:, : LANES // 2]], axis=1)
    keys = (keys * cosine_ref[...] + turned * sine_ref[...]).astype(jnp.bfloat16)
    count = query_ref.shape[0]
    fresh = lax.dot_general(
        query_ref[...], keys, (((1,), (1,)), ((), ())), preferred_element_type=jnp.float32
    ) * (HEAD_SIZE**-0.5)
    row = lax.broadcasted_iota(jnp.int32, fresh.shape, 0)
    column = lax.broadcasted_iota(jnp.int32, fresh.shape, 1)
    each = count // (tokens // 2)
    step = row % each // (each // 2)
    rollouts = tokens // 2
    joined = (row // each == column % rollouts) & (column // rollouts <= step)
    fresh = jnp.where(joined, fresh, -jnp.inf)
    highest = jnp.maximum(highest_ref[...], jnp.max(fresh, axis=-1, keepdims=True))
    weights = jnp.exp(fresh - highest)
    factor = jnp.exp(highest_ref[...] - highest)
    denominator = sum_ref[...] * factor + jnp.sum(weights, axis=-1, keepdims=True)
    mixed = mixed_ref[...] * factor + jnp.dot(
        weights,
        values.astype(jnp.float32),
        precision=lax.Precision.HIGHEST,
        preferred_element_type=jnp.float32,
    )
    mixed = (mixed / denominator).astype(jnp.bfloat16)
    groups = each // 2
    for at in range(2 * out_ref.shape[0]):
        for group in range(groups):
            out_ref[at // 2, at % 2 : at % 2 + 1, group * HEAD_SIZE : (group + 1) * HEAD_SIZE] = (
                mixed[at * groups + group : at * groups + group + 1, :]
            )


FEATURES = 5120


def body(
    token_ids,
    cache_lengths,
    embedding,
    norm_gain,
    key_norm_gain,
    key_weight,
    key_grad,
    key_first,
    key_second,
    value_weight,
    value_grad,
    value_first,
    value_second,
    queries,
    key_cache,
    cached_value_rows,
):
    rollouts = token_ids.shape[0]
    tokens = 2 * rollouts
    z_size, quad_size, tp_size = lax.axis_size("z"), lax.axis_size(QUAD), lax.axis_size(TP)
    own_rows = key_weight.shape[0]
    vocab_rows, features = embedding.shape

    chips = z_size * lax.axis_size("xh")
    own_ids = jnp.broadcast_to(token_ids.T[None], (chips, 2, rollouts))
    all_ids = lax.all_to_all(own_ids, ("xh", "z"), split_axis=0, concat_axis=0, tiled=False)

    sort = pl.pallas_call(
        sort_columns,
        out_shape=jax.ShapeDtypeStruct((features, 2 * CHUNK), jnp.bfloat16),
        compiler_params=pltpu.CompilerParams(vmem_limit_bytes=4 * 1024 * 1024),
        cost_estimate=pl.CostEstimate(
            flops=COVER_FLOPS, bytes_accessed=COVER_BYTES, transcendentals=0
        ),
    )()
    all_ids, sort = lax.optimization_barrier((all_ids, sort))
    other = lax.ppermute(embedding, "core", [(0, 1), (1, 0)])

    part = lax.axis_index(FSDP)
    ids = all_ids.reshape(1, -1)
    own_row, other_row = ids - part * vocab_rows, ids - (part ^ 1) * vocab_rows
    row = jnp.where((own_row >= 0) & (own_row < vocab_rows), own_row, -1)
    row = jnp.where((other_row >= 0) & (other_row < vocab_rows), other_row + vocab_rows, row)
    found = call(look_up, (row.shape[1], features), jnp.bfloat16, row, embedding, other)

    (
        found,
        key_weight,
        key_grad,
        key_first,
        key_second,
        value_weight,
        value_grad,
        value_first,
        value_second,
        cache_lengths,
        key_norm_gain,
        norm_gain,
    ) = lax.optimization_barrier(
        (
            found,
            key_weight,
            key_grad,
            key_first,
            key_second,
            value_weight,
            value_grad,
            value_first,
            value_second,
            cache_lengths,
            key_norm_gain,
            norm_gain,
        )
    )

    state = jax.ShapeDtypeStruct(key_weight.shape, jnp.float32)
    (
        new_key_weight,
        new_key_first,
        new_key_second,
        new_value_weight,
        new_value_first,
        new_value_second,
        both,
    ) = pl.pallas_call(
        update,
        out_shape=[state] * 6
        + [jax.ShapeDtypeStruct((own_rows, 2 * tp_size * HEAD_SIZE), jnp.bfloat16)],
        compiler_params=pltpu.CompilerParams(vmem_limit_bytes=4 * 1024 * 1024),
        cost_estimate=pl.CostEstimate(
            flops=COVER_FLOPS, bytes_accessed=COVER_BYTES, transcendentals=0
        ),
    )(
        key_weight,
        key_grad,
        key_first,
        key_second,
        value_weight,
        value_grad,
        value_first,
        value_second,
    )
    quad_rows = lax.all_gather(both, QUAD, axis=0, tiled=False)
    quad_rows = quad_rows.reshape(quad_size * own_rows, tp_size, 2 * HEAD_SIZE).transpose(1, 0, 2)
    quad_rows = jnp.pad(quad_rows, ((0, 0), (0, BLOCK - BLOCK_ROWS), (0, 0)))

    gain = jnp.dot(
        norm_gain.reshape(z_size, -1), sort[: features // 2, :CHUNK], preferred_element_type=jnp.float32
    )
    gain = lax.dynamic_slice_in_dim(gain, lax.axis_index("z"), 1, axis=0)

    groups = queries.shape[2] // HEAD_SIZE
    slots = key_cache.shape[2]
    score_scale = HEAD_SIZE ** (-0.5)
    rows = queries.reshape(rollouts, 2 * groups, HEAD_SIZE)
    cache_scores = (
        jnp.einsum("rqd,rcd->rqc", rows, key_cache[:, 0], preferred_element_type=jnp.float32)
        * score_scale
    )
    valid_cache = jnp.arange(slots, dtype=jnp.int32)[None, :] < cache_lengths[:, None]
    cache_scores = jnp.where(valid_cache[:, None, :], cache_scores, -jnp.inf)
    cache_highest = jnp.max(cache_scores, axis=-1, keepdims=True)
    cache_exp = jnp.exp(cache_scores - cache_highest)
    cache_sum = jnp.sum(cache_exp, axis=-1, keepdims=True)
    high = lax.reduce_precision(cache_exp, 8, 7)
    low = (cache_exp - high).astype(jnp.bfloat16)
    high = high.astype(jnp.bfloat16)
    cache_mixed = jnp.einsum(
        "rqc,rcd->rqd",
        jnp.concatenate([high, low], axis=1),
        cached_value_rows[:, 0],
        preferred_element_type=jnp.float32,
    )
    cache_mixed = cache_mixed[:, : 2 * groups] + cache_mixed[:, 2 * groups :]

    positions = (cache_lengths[None, :] + jnp.arange(2, dtype=jnp.int32)[:, None]).astype(
        jnp.float32
    )
    frequency = rope_base ** (
        -jnp.arange(HEAD_SIZE // 2, dtype=jnp.float32) * 2.0 / HEAD_SIZE
    )
    angles = positions.reshape(tokens, 1) * frequency
    cosine, sine = jnp.cos(angles), jnp.sin(angles)
    cosine = jnp.concatenate([cosine, cosine], axis=1)
    sine = jnp.concatenate([-sine, sine], axis=1)

    each = 2 * tokens
    found = found.reshape(-1, each, features)
    found = lax.all_to_all(found, ("xh", TP), split_axis=0, concat_axis=0, tiled=False)
    found = found.reshape(2, tp_size, each, features)
    found = call(split_rows, (z_size, each, CHUNK), jnp.bfloat16, found, sort)
    found = lax.all_to_all(found, "z", split_axis=0, concat_axis=0, tiled=False)
    message_rows = CHUNK // LANES * each + 2 * BLOCK
    packed = call(pack, (tp_size, message_rows, LANES), jnp.bfloat16, found, quad_rows)
    packed = lax.all_to_all(packed, TP, split_axis=0, concat_axis=0, tiled=False)
    product = call(project, (z_size, 2 * tokens, HEAD_SIZE), jnp.bfloat16, packed, gain)
    product = lax.all_to_all(product, "z", split_axis=0, concat_axis=0, tiled=False)
    attention = call(
        finish,
        queries.shape,
        jnp.bfloat16,
        product,
        key_norm_gain.astype(jnp.float32).reshape(1, HEAD_SIZE),
        cosine,
        sine,
        rows.reshape(-1, HEAD_SIZE),
        cache_mixed.reshape(-1, HEAD_SIZE),
        cache_highest.reshape(-1, 1),
        cache_sum.reshape(-1, 1),
    )
    return (
        attention,
        new_key_weight,
        new_key_first,
        new_key_second,
        new_value_weight,
        new_value_first,
        new_value_second,
    )


QUAD = ("xh", "core")
FSDP = ("z", "xh", "core")
TP = "tp"


def solution(mesh):
    fine = Mesh(mesh.devices.reshape(16, 2, 2, 8), ("z", "xh", "core", "tp"))
    rows = P(FSDP + (TP,), None)
    placed = (
        P(FSDP, None),
        P(FSDP),
        P(FSDP, TP),
        P(),
        P(),
        *[rows] * 8,
        P(FSDP, None, TP),
        P(FSDP, TP, None, None),
        P(FSDP, TP, None, None),
    )
    return jax.shard_map(
        body,
        mesh=fine,
        in_specs=placed,
        out_specs=(P(FSDP, None, TP), *[rows] * 6),
        check_vma=False,
    )
```

```python
import jax
import jax.numpy as jnp
from jax import lax
from jax.experimental import pallas as pl
from jax.experimental.pallas import tpu as pltpu
from jax.sharding import Mesh
from jax.sharding import PartitionSpec as P

HEAD_SIZE = 128
LANES = 128
BLOCK_ROWS = 40
BLOCK = 48
CHUNK = 384
OWN_ROWS = 10
COVER_FLOPS = 20_000_000_000
COVER_BYTES = 60_000_000
HIGH_COLUMN = 40
LOW_COLUMN = 41


beta_one = 0.9
beta_two = 0.95
learn_rate = 0.001
weight_decay = 0.1
adam_eps = 1e-08
norm_eps = 1e-06
rope_base = 1000000.0


def adamw(weight, gradient, moment_one, moment_two):
    first_new = beta_one * moment_one + (1.0 - beta_one) * gradient
    second_new = beta_two * moment_two + (1.0 - beta_two) * gradient * gradient
    correct_one = 1.0 - beta_one**50
    correct_two = 1.0 - beta_two**50
    update = (
        first_new / correct_one / (jnp.sqrt(second_new / correct_two) + adam_eps)
        + weight_decay * weight
    )
    return (weight - learn_rate * update, first_new, second_new)


def call(kernel, shape, dtype, *operands):
    return pl.pallas_call(
        kernel,
        out_shape=jax.ShapeDtypeStruct(shape, dtype),
        compiler_params=pltpu.CompilerParams(vmem_limit_bytes=16 * 1024 * 1024),
    )(*operands)


def look_up(row_ref, table_ref, other_ref, found_ref):
    count = row_ref.shape[1]
    eye = lax.broadcasted_iota(jnp.int32, (count, count), 0) == lax.broadcasted_iota(
        jnp.int32, (count, count), 1
    )
    row = jnp.broadcast_to(row_ref[...], (count, count))
    row = jnp.sum(jnp.where(eye, row, 0), axis=1, keepdims=True)
    size = table_ref.shape[0]
    index = lax.broadcasted_iota(jnp.int32, (count, size), 1)
    own = jnp.where(row == index, 1.0, 0.0).astype(jnp.bfloat16)
    other = jnp.where(row - size == index, 1.0, 0.0).astype(jnp.bfloat16)
    total = jnp.dot(own, table_ref[...], preferred_element_type=jnp.float32)
    total += jnp.dot(other, other_ref[...], preferred_element_type=jnp.float32)
    found_ref[...] = total.astype(jnp.bfloat16)


def update(*refs):
    given, new, both_ref = refs[:8], refs[8:14], refs[14]
    for side in range(2):
        results = adamw(*[ref[...] for ref in given[4 * side : 4 * side + 4]])
        for ref, result in zip(new[3 * side : 3 * side + 3], results):
            ref[...] = result
        rounded = results[0].astype(jnp.bfloat16)
        for place in range(rounded.shape[1] // HEAD_SIZE):
            start = (2 * place + side) * HEAD_SIZE
            both_ref[:, start : start + HEAD_SIZE] = rounded[
                :, place * HEAD_SIZE : (place + 1) * HEAD_SIZE
            ]


def sort_columns(sort_ref):
    features = sort_ref.shape[0]
    column = lax.broadcasted_iota(jnp.int32, sort_ref.shape, 1)
    half, place, row = column // CHUNK, column % CHUNK // BLOCK, column % BLOCK
    quad, own = row // OWN_ROWS, row % OWN_ROWS
    feature = half * (features // 2) + (quad * (CHUNK // BLOCK) + place) * OWN_ROWS + own
    held = lax.broadcasted_iota(jnp.int32, sort_ref.shape, 0)
    chosen = (held == feature) & (row < BLOCK_ROWS)
    sort_ref[...] = jnp.where(chosen, 1.0, 0.0).astype(jnp.bfloat16)


def split_rows(came_ref, sort_ref, chunks_ref):
    total = came_ref[0].astype(jnp.float32) + came_ref[1].astype(jnp.float32)
    places, count, features = total.shape
    squares = jnp.sum(jnp.sum(total * total, axis=0), axis=-1, keepdims=True)
    high = squares.astype(jnp.bfloat16).astype(jnp.float32)
    low = squares - high
    column = lax.broadcasted_iota(jnp.int32, (count, CHUNK), 1)
    extra = jnp.where(column == HIGH_COLUMN, high, jnp.where(column == LOW_COLUMN, low, 0.0))
    total = total.reshape(places * count, features).astype(jnp.bfloat16)
    total = jnp.dot(total, sort_ref[...], preferred_element_type=jnp.float32)
    total = total.reshape(places, count, 2 * CHUNK)
    for place in range(places):
        for half in range(2):
            chunk = total[place, :, half * CHUNK : (half + 1) * CHUNK] + extra
            chunks_ref[2 * place + half] = chunk.astype(jnp.bfloat16)


def pack(came_ref, weight_ref, packed_ref):
    rows = jnp.sum(came_ref[...].astype(jnp.float32), axis=0).astype(jnp.bfloat16)
    count = rows.shape[0]
    parts = CHUNK // LANES
    for place in range(packed_ref.shape[0]):
        for part in range(parts):
            packed_ref[place, part * count : (part + 1) * count, :] = rows[
                :, part * LANES : (part + 1) * LANES
            ]
        packed_ref[place, parts * count : parts * count + BLOCK, :] = weight_ref[place, :, :LANES]
        packed_ref[place, parts * count + BLOCK :, :] = weight_ref[place, :, LANES:]


def project(came_ref, gain_ref, product_ref):
    places = came_ref.shape[0]
    parts = CHUNK // LANES
    count = (came_ref.shape[1] - 2 * BLOCK) // parts
    rows = [
        came_ref[:, part * count : (part + 1) * count, :]
        .reshape(places * count, LANES)
        .astype(jnp.float32)
        for part in range(parts)
    ]
    column = lax.broadcasted_iota(jnp.int32, rows[0].shape, 1)
    marked = (column == HIGH_COLUMN) | (column == LOW_COLUMN)
    squares = jnp.sum(jnp.where(marked, rows[0], 0.0), axis=-1, keepdims=True)
    factor = lax.rsqrt(squares / FEATURES + norm_eps)
    normed = jnp.concatenate(
        [
            (rows[part] * factor * gain_ref[:, part * LANES : (part + 1) * LANES]).astype(
                jnp.bfloat16
            )
            for part in range(parts)
        ],
        axis=1,
    )
    products = []
    for side in range(2):
        start = parts * count + side * BLOCK
        weight = came_ref[:, start : start + BLOCK, :].reshape(places * BLOCK, LANES)
        product = jnp.dot(normed, weight, preferred_element_type=jnp.float32)
        products.append(product.reshape(product_ref.shape[0], product_ref.shape[1] // 2, LANES))
    product_ref[...] = jnp.concatenate(products, axis=1).astype(jnp.bfloat16)


def finish(
    came_ref, gain_ref, cosine_ref, sine_ref, query_ref, mixed_ref, highest_ref, sum_ref, out_ref
):
    total = jnp.sum(came_ref[...].astype(jnp.float32), axis=0)
    tokens = total.shape[0] // 2
    keys = total[:tokens]
    values = total[tokens:].astype(jnp.bfloat16)
    factor = lax.rsqrt(jnp.mean(keys * keys, axis=-1, keepdims=True) + norm_eps)
    keys = keys * factor * gain_ref[...]
    turned = jnp.concatenate([keys[:, LANES // 2 :], keys[:, : LANES // 2]], axis=1)
    keys = (keys * cosine_ref[...] + turned * sine_ref[...]).astype(jnp.bfloat16)
    count = query_ref.shape[0]
    fresh = lax.dot_general(
        query_ref[...], keys, (((1,), (1,)), ((), ())), preferred_element_type=jnp.float32
    ) * (HEAD_SIZE**-0.5)
    row = lax.broadcasted_iota(jnp.int32, fresh.shape, 0)
    column = lax.broadcasted_iota(jnp.int32, fresh.shape, 1)
    each = count // (tokens // 2)
    step = row % each // (each // 2)
    rollouts = tokens // 2
    joined = (row // each == column % rollouts) & (column // rollouts <= step)
    fresh = jnp.where(joined, fresh, -jnp.inf)
    highest = jnp.maximum(highest_ref[...], jnp.max(fresh, axis=-1, keepdims=True))
    weights = jnp.exp(fresh - highest)
    factor = jnp.exp(highest_ref[...] - highest)
    denominator = sum_ref[...] * factor + jnp.sum(weights, axis=-1, keepdims=True)
    mixed = mixed_ref[...] * factor + jnp.dot(
        weights,
        values.astype(jnp.float32),
        precision=lax.Precision.HIGHEST,
        preferred_element_type=jnp.float32,
    )
    mixed = (mixed / denominator).astype(jnp.bfloat16)
    groups = each // 2
    for at in range(2 * out_ref.shape[0]):
        for group in range(groups):
            out_ref[at // 2, at % 2 : at % 2 + 1, group * HEAD_SIZE : (group + 1) * HEAD_SIZE] = (
                mixed[at * groups + group : at * groups + group + 1, :]
            )


FEATURES = 5120


def body(
    token_ids,
    cache_lengths,
    embedding,
    norm_gain,
    key_norm_gain,
    key_weight,
    key_grad,
    key_first,
    key_second,
    value_weight,
    value_grad,
    value_first,
    value_second,
    queries,
    key_cache,
    cached_value_rows,
):
    rollouts = token_ids.shape[0]
    tokens = 2 * rollouts
    z_size, quad_size, tp_size = lax.axis_size("z"), lax.axis_size(QUAD), lax.axis_size(TP)
    own_rows = key_weight.shape[0]
    vocab_rows, features = embedding.shape

    chips = z_size * lax.axis_size("xh")
    own_ids = jnp.broadcast_to(token_ids.T[None], (chips, 2, rollouts))
    all_ids = lax.all_to_all(own_ids, ("xh", "z"), split_axis=0, concat_axis=0, tiled=False)

    sort = pl.pallas_call(
        sort_columns,
        out_shape=jax.ShapeDtypeStruct((features, 2 * CHUNK), jnp.bfloat16),
        compiler_params=pltpu.CompilerParams(vmem_limit_bytes=4 * 1024 * 1024),
        cost_estimate=pl.CostEstimate(
            flops=COVER_FLOPS, bytes_accessed=COVER_BYTES, transcendentals=0
        ),
    )()
    all_ids, sort = lax.optimization_barrier((all_ids, sort))
    other = lax.ppermute(embedding, "core", [(0, 1), (1, 0)])

    part = lax.axis_index(FSDP)
    ids = all_ids.reshape(1, -1)
    own_row, other_row = ids - part * vocab_rows, ids - (part ^ 1) * vocab_rows
    row = jnp.where((own_row >= 0) & (own_row < vocab_rows), own_row, -1)
    row = jnp.where((other_row >= 0) & (other_row < vocab_rows), other_row + vocab_rows, row)
    found = call(look_up, (row.shape[1], features), jnp.bfloat16, row, embedding, other)

    (
        found,
        key_weight,
        key_grad,
        key_first,
        key_second,
        value_weight,
        value_grad,
        value_first,
        value_second,
        cache_lengths,
        key_norm_gain,
        norm_gain,
    ) = lax.optimization_barrier(
        (
            found,
            key_weight,
            key_grad,
            key_first,
            key_second,
            value_weight,
            value_grad,
            value_first,
            value_second,
            cache_lengths,
            key_norm_gain,
            norm_gain,
        )
    )

    state = jax.ShapeDtypeStruct(key_weight.shape, jnp.float32)
    (
        new_key_weight,
        new_key_first,
        new_key_second,
        new_value_weight,
        new_value_first,
        new_value_second,
        both,
    ) = pl.pallas_call(
        update,
        out_shape=[state] * 6
        + [jax.ShapeDtypeStruct((own_rows, 2 * tp_size * HEAD_SIZE), jnp.bfloat16)],
        compiler_params=pltpu.CompilerParams(vmem_limit_bytes=4 * 1024 * 1024),
        cost_estimate=pl.CostEstimate(
            flops=COVER_FLOPS, bytes_accessed=COVER_BYTES, transcendentals=0
        ),
    )(
        key_weight,
        key_grad,
        key_first,
        key_second,
        value_weight,
        value_grad,
        value_first,
        value_second,
    )
    pair_rows = lax.all_gather(both, "core", axis=0, tiled=False)
    gain = jnp.dot(
        norm_gain.reshape(z_size, -1), sort[: features // 2, :CHUNK], preferred_element_type=jnp.float32
    )
    gain = lax.dynamic_slice_in_dim(gain, lax.axis_index("z"), 1, axis=0)

    groups = queries.shape[2] // HEAD_SIZE
    slots = key_cache.shape[2]
    score_scale = HEAD_SIZE ** (-0.5)
    rows = queries.reshape(rollouts, 2 * groups, HEAD_SIZE)
    cache_scores = (
        jnp.einsum("rqd,rcd->rqc", rows, key_cache[:, 0], preferred_element_type=jnp.float32)
        * score_scale
    )
    valid_cache = jnp.arange(slots, dtype=jnp.int32)[None, :] < cache_lengths[:, None]
    cache_scores = jnp.where(valid_cache[:, None, :], cache_scores, -jnp.inf)
    cache_highest = jnp.max(cache_scores, axis=-1, keepdims=True)
    cache_exp = jnp.exp(cache_scores - cache_highest)
    cache_sum = jnp.sum(cache_exp, axis=-1, keepdims=True)
    high = lax.reduce_precision(cache_exp, 8, 7)
    low = (cache_exp - high).astype(jnp.bfloat16)
    high = high.astype(jnp.bfloat16)
    cache_mixed = jnp.einsum(
        "rqc,rcd->rqd",
        jnp.concatenate([high, low], axis=1),
        cached_value_rows[:, 0],
        preferred_element_type=jnp.float32,
    )
    cache_mixed = cache_mixed[:, : 2 * groups] + cache_mixed[:, 2 * groups :]

    positions = (cache_lengths[None, :] + jnp.arange(2, dtype=jnp.int32)[:, None]).astype(
        jnp.float32
    )
    frequency = rope_base ** (
        -jnp.arange(HEAD_SIZE // 2, dtype=jnp.float32) * 2.0 / HEAD_SIZE
    )
    angles = positions.reshape(tokens, 1) * frequency
    cosine, sine = jnp.cos(angles), jnp.sin(angles)
    cosine = jnp.concatenate([cosine, cosine], axis=1)
    sine = jnp.concatenate([-sine, sine], axis=1)

    each = 2 * tokens
    found = found.reshape(-1, each, features)
    found = lax.all_to_all(found, ("xh", TP), split_axis=0, concat_axis=0, tiled=False)
    found, pair_rows = lax.optimization_barrier((found, pair_rows))
    quad_rows = lax.all_gather(pair_rows, "xh", axis=0, tiled=False)
    quad_rows = quad_rows.reshape(quad_size * own_rows, tp_size, 2 * HEAD_SIZE).transpose(1, 0, 2)
    quad_rows = jnp.pad(quad_rows, ((0, 0), (0, BLOCK - BLOCK_ROWS), (0, 0)))

    found = found.reshape(2, tp_size, each, features)
    found = call(split_rows, (z_size, each, CHUNK), jnp.bfloat16, found, sort)
    found = lax.all_to_all(found, "z", split_axis=0, concat_axis=0, tiled=False)
    message_rows = CHUNK // LANES * each + 2 * BLOCK
    packed = call(pack, (tp_size, message_rows, LANES), jnp.bfloat16, found, quad_rows)
    packed = lax.all_to_all(packed, TP, split_axis=0, concat_axis=0, tiled=False)
    product = call(project, (z_size, 2 * tokens, HEAD_SIZE), jnp.bfloat16, packed, gain)
    product = lax.all_to_all(product, "z", split_axis=0, concat_axis=0, tiled=False)
    attention = call(
        finish,
        queries.shape,
        jnp.bfloat16,
        product,
        key_norm_gain.astype(jnp.float32).reshape(1, HEAD_SIZE),
        cosine,
        sine,
        rows.reshape(-1, HEAD_SIZE),
        cache_mixed.reshape(-1, HEAD_SIZE),
        cache_highest.reshape(-1, 1),
        cache_sum.reshape(-1, 1),
    )
    return (
        attention,
        new_key_weight,
        new_key_first,
        new_key_second,
        new_value_weight,
        new_value_first,
        new_value_second,
    )


QUAD = ("xh", "core")
FSDP = ("z", "xh", "core")
TP = "tp"


def solution(mesh):
    fine = Mesh(mesh.devices.reshape(16, 2, 2, 8), ("z", "xh", "core", "tp"))
    rows = P(FSDP + (TP,), None)
    placed = (
        P(FSDP, None),
        P(FSDP),
        P(FSDP, TP),
        P(),
        P(),
        *[rows] * 8,
        P(FSDP, None, TP),
        P(FSDP, TP, None, None),
        P(FSDP, TP, None, None),
    )
    return jax.shard_map(
        body,
        mesh=fine,
        in_specs=placed,
        out_specs=(P(FSDP, None, TP), *[rows] * 6),
        check_vma=False,
    )
```
